768 devices in a mesh: node: 96 (over x, z, core), local: 8 (over y).
Axes of the slice: x: 4, y: 8, z: 12, core: 2. Of those that a mesh axis runs over, the one named last changes fastest.
Arguments:
- image: float32 [12288, 128], P(('node', 'local')), may hold values from -6 to 6
- direction: float32 [12288, 128], P(('node', 'local')), may hold values from -60 to 60
- gradient: float32 [12288, 128], P(('node', 'local')), may hold values from -60 to 60
- residual: float32 [6144, 128], P(('node', 'local')), may hold values from -6 to 6
- blocks: bfloat16 [24576, 128, 128], P(('node', 'local')), may hold values from -0.25 to 0.25
- block_slot: int32 [24576], P(('node', 'local')), may hold values from 0 to 767
- block_pixel: int32 [24576], P(('node', 'local')), may hold values from 0 to 15
- slot_ray: int32 [73728], P(('node', 'local')), may hold values from 0 to 6143, as said below
Outputs:
- new_image: float32 [12288, 128], P(('node', 'local'))
- new_residual: float32 [6144, 128], P(('node', 'local'))
- new_direction: float32 [12288, 128], P(('node', 'local'))
The draws below stay inside these ranges and needn't reach their ends.
Inputs may be any that keep to these rules, and one draw needn't show every extreme that they name: `slot_ray`: slot j of device d (entry d * 96 + j) names a ray tile owned by a device with the same index along local as d (ray tile t is owned by device t // 8). From one device at most 2 slots name ray tiles owned by the devices of one index along node, exactly 2 for some index, and for every index along local some owner receives exactly 2 slots from every device of that local index.
All inputs are finite; a program needn't handle non-finite values.
Results may differ from the reference program's by a relative error of at most 0.0028.
Values may be sent and summed in bfloat16 or wider, within the bound.
A program may use at most 32 MiB of HBM per device.

```python
import jax
import jax.numpy as jnp
from jax import lax

PT = 128
RT = 128
SEND_CAPACITY = 2
PTD = 16
RAY_TILES_OWNED = 8
BLK = 32
GROUP_SLOTS_HELD = 96
GS = 768
NPT = 12288
NRT = 6144
NB = 24576
N_NODE = 96
N_LOCAL = 8
DEVICES = 768


def field_scale(key_scale):
    key_tile_draw, key_column = jax.random.split(key_scale, 2)
    tile_scale = jnp.exp(jax.random.uniform(key_tile_draw, (NPT, 1), dtype=jnp.float32) * jnp.log(3.1623))
    column_scale = jnp.exp(jax.random.uniform(key_column, (1, PT), dtype=jnp.float32) * jnp.log(3.1623))
    rising = 1.0 + 2.0 * jnp.arange(NPT, dtype=jnp.float32)[:, None] / max(NPT - 1, 1)
    return 0.3 * rising * tile_scale * column_scale


def draw_direction(key, part):
    key = jax.random.fold_in(key, 11)
    key_scale = jax.random.fold_in(key, 0)
    key_noise = jax.random.fold_in(key, 2)
    scale_field = field_scale(key_scale)
    base_field = jnp.clip(jax.random.normal(key_noise, (NPT, PT), dtype=jnp.float32), -6.0, 6.0)
    return (scale_field * base_field).astype(jnp.float32)


def draw_gradient(key, part):
    key = jax.random.fold_in(key, 23)
    key_scale = jax.random.fold_in(key, 0)
    key_noise = jax.random.fold_in(key, 2)
    scale_field = field_scale(key_scale)
    base_field = jnp.clip(jax.random.normal(key_noise, (NPT, PT), dtype=jnp.float32), -6.0, 6.0)
    return (scale_field * base_field).astype(jnp.float32)


def draw_slot_ray(key, part):
    key = jax.random.fold_in(key, 5)
    key_full, key_shuffle, key_permute, key_tile_draw = jax.random.split(key, 4)
    full_node = jax.random.randint(key_full, (N_LOCAL,), 0, N_NODE)
    holder = jnp.arange(DEVICES, dtype=jnp.int32)
    local_of = holder % N_LOCAL
    full_of = full_node[local_of]
    spare_count = (N_NODE - 1) * SEND_CAPACITY
    first_node = jnp.arange(spare_count, dtype=jnp.int32) // SEND_CAPACITY
    permuted_tiles = jax.vmap(lambda lone_entry: jax.random.permutation(lone_entry, spare_count))(jax.random.split(key_shuffle, DEVICES))
    selected_tiles = first_node[permuted_tiles[:, :GROUP_SLOTS_HELD - SEND_CAPACITY]]
    selected_tiles = selected_tiles + (selected_tiles >= full_of[:, None]).astype(jnp.int32)
    target_node = jnp.concatenate([jnp.broadcast_to(full_of[:, None], (DEVICES, SEND_CAPACITY)), selected_tiles], axis=1)
    tile_permutation = jax.vmap(lambda lone_entry: jax.random.permutation(lone_entry, GROUP_SLOTS_HELD))(jax.random.split(key_permute, DEVICES))
    target_node = jnp.take_along_axis(target_node, tile_permutation, axis=1)
    tile_position = jax.random.randint(key_tile_draw, (DEVICES, GROUP_SLOTS_HELD), 0, RAY_TILES_OWNED)
    ray_index = (target_node * N_LOCAL + local_of[:, None]) * RAY_TILES_OWNED + tile_position
    return ray_index.reshape(-1).astype(jnp.int32)


def touch_ends(values, own_key, low, high):
    longest = values.shape.index(max(values.shape))
    spots = []
    for shift in (0, 1):
        where = [jax.random.randint(jax.random.fold_in(own_key, axis), (), 0, length) for axis, length in enumerate(values.shape)]
        where[longest] = (where[longest] + shift) % values.shape[longest]
        spots.append(tuple(where))
    return values.at[spots[0]].set(low).at[spots[1]].set(high)


def level_of(key, extent, shards, least, largest):
    gain = 1.0
    for position, shards_of in shards:
        draws = jax.random.uniform(jax.random.fold_in(jax.random.fold_in(key, 6), position), (shards_of,), jnp.float32, least / len(shards), largest / len(shards))
        gain = gain * jnp.repeat(jnp.exp(draws), extent[position] // shards_of).reshape((-1,) + (1,) * (len(extent) - 1 - position))
    return gain


def bell_draw(rng, extent, width, limit, pieces=(), kind=jnp.bfloat16):
    factor_of = level_of(rng, extent, pieces, -0.22, 0.18) if pieces else 1.0
    result = jax.random.normal(rng, extent, jnp.float32) * width * factor_of
    return jnp.minimum(jnp.maximum(result, -limit), limit).astype(kind)


def setup_inputs(seed: int = 0) -> dict:
    key_of = jax.random.split(jax.random.key(seed), 9)
    image = bell_draw(key_of[0], (NPT, PT), 0.5, 6.0, ((0, 768),), jnp.float32)
    direction = draw_direction(jax.random.fold_in(key_of[8], 71), 0)
    gradient = draw_gradient(jax.random.fold_in(key_of[8], 71), 0)
    residual = bell_draw(key_of[3], (NRT, RT), 1.0, 6.0, ((0, 768),), jnp.float32)
    blocks = bell_draw(key_of[4], (NB, RT, PT), (PT * BLK // RAY_TILES_OWNED) ** -0.5, 0.25, ((0, 768),))
    block_slot = touch_ends(jax.random.randint(key_of[5], (NB,), 0, GS), jax.random.fold_in(key_of[5], 1), 0, GS - 1).astype(jnp.int32)
    block_pixel = touch_ends(jax.random.randint(key_of[6], (NB,), 0, PTD), jax.random.fold_in(key_of[6], 1), 0, PTD - 1).astype(jnp.int32)
    slot_ray = draw_slot_ray(jax.random.fold_in(key_of[8], 71), 0)
    return {"image": image, "direction": direction, "gradient": gradient, "residual": residual, "blocks": blocks, "block_slot": block_slot, "block_pixel": block_pixel, "slot_ray": slot_ray}


def forward_tiles(operands):
    return jnp.einsum("brp,bp->br", operands[0].astype(jnp.float32), operands[1].astype(jnp.float32), precision=lax.Precision.HIGHEST)


def backward_tiles(operands):
    return jnp.einsum("brp,br->bp", operands[0].astype(jnp.float32), operands[1].astype(jnp.float32), precision=lax.Precision.HIGHEST)


def reference(image, direction, gradient, residual, blocks, block_slot, block_pixel, slot_ray):
    old_norm = jnp.sum(gradient * gradient)
    block_total = blocks.shape[0]
    device_of = jnp.arange(block_total, dtype=jnp.int32) // BLK
    group_of = device_of // N_LOCAL
    ray_of = slot_ray[(group_of * GS + block_slot).astype(jnp.int32)]
    pixel_of = (device_of * PTD + block_pixel).astype(jnp.int32)
    low_direction = direction.astype(jnp.bfloat16)
    tile_blocks = blocks.reshape(DEVICES, BLK, RT, PT)
    selected_tiles = low_direction[pixel_of].reshape(DEVICES, BLK, PT)
    contrib = lax.map(forward_tiles, (tile_blocks, selected_tiles)).reshape(block_total, RT)
    projected = jax.ops.segment_sum(contrib, ray_of, num_segments=NRT)
    curvature = jnp.sum(projected * projected)
    step_size = old_norm / curvature
    new_image = image + step_size * direction
    new_residual = residual - step_size * projected
    low_residual = new_residual.astype(jnp.bfloat16)
    chosen = low_residual[ray_of].reshape(DEVICES, BLK, RT)
    backward = lax.map(backward_tiles, (tile_blocks, chosen)).reshape(block_total, PT)
    gradient_new = jax.ops.segment_sum(backward, pixel_of, num_segments=NPT)
    new_norm = jnp.sum(gradient_new * gradient_new)
    new_direction = gradient_new + (new_norm / old_norm) * direction
    return new_image, new_residual, new_direction
```

```python
import functools

import jax
import jax.numpy as jnp
from jax import lax
from jax.experimental import pallas as pl
from jax.experimental.pallas import tpu as pltpu
from jax.sharding import PartitionSpec as P

SEND_CAPACITY = 2
LANES = 128
MESH = pl.DeviceIdType.MESH
NT = (((1,), (1,)), ((), ()))


def iota(shape, axis):
    return lax.broadcasted_iota(jnp.int32, shape, axis)


def dot(a, b, dims=(((1,), (0,)), ((), ()))):
    return lax.dot_general(a, b, dims, preferred_element_type=jnp.float32)


def one_hot_dot(one_hot, value):
    high = value.astype(jnp.bfloat16)
    rest = value - high.astype(jnp.float32)
    middle = rest.astype(jnp.bfloat16)
    low = (rest - middle.astype(jnp.float32)).astype(jnp.bfloat16)
    width = value.shape[1]
    out = dot(one_hot, jnp.concatenate([high, middle, low], axis=1))
    return out[:, :width] + (out[:, width : 2 * width] + out[:, 2 * width :])


def to_column(row):
    length = row.shape[1]
    square = (length, length)
    return jnp.sum(jnp.where(iota(square, 0) == iota(square, 1), row, 0.0), axis=1, keepdims=True)


def kernel(
    sizes,
    image_hbm, direction_hbm, gradient_hbm, residual_hbm, blocks_hbm, slot_hbm, pixel_hbm, ray_hbm,
    image_out, residual_out, direction_out,
    image, direction, gradient, residual, blocks, slot, pixel, ray, load_sem,
    slot_send, slot_recv, label_send, label_recv,
    contrib_send, contrib_recv, held_send, held_recv,
    reply_send, reply_recv, chosen_send, chosen_recv,
    early_send, early_recv, early_chosen_send, early_chosen_recv,
    norm_a_send, norm_a_recv, norm_b_send, norm_b_recv,
    last_a_send, last_a_recv, last_b_send, last_b_recv,
    y_send_sem, y_recv_sem, n_send_sem, n_recv_sem, s_send_sem, s_recv_sem,
):
    node_count, local_count, row_count = sizes
    column_count = node_count // row_count
    node = lax.axis_index("node")
    local = lax.axis_index("local")
    row = node // column_count
    column = lax.rem(node, column_count)
    tiles, block_count = image.shape[0], blocks.shape[0]
    held, owned = ray.shape[1], residual.shape[0]
    rows_sent = node_count * SEND_CAPACITY
    group_blocks = block_count * local_count

    chunks = 4
    chunk = block_count // chunks
    loads = {}
    for index, (name, source, target) in enumerate(
        (
            ("ray", ray_hbm, ray),
            ("direction", direction_hbm, direction),
            ("pixel", pixel_hbm, pixel),
            ("slot", slot_hbm, slot),
            *(
                (("blocks", c), blocks_hbm.at[pl.ds(c * chunk, chunk)], blocks.at[pl.ds(c * chunk, chunk)])
                for c in range(chunks)
            ),
            ("gradient", gradient_hbm, gradient),
            ("residual", residual_hbm, residual),
            ("image", image_hbm, image),
        )
    ):
        loads[name] = pltpu.make_async_copy(source, target, load_sem.at[index])
        loads[name].start()

    def of_local(k):
        other = lax.rem(local + k, local_count)
        return other, (node, other)

    def of_node(k):
        other = lax.rem(node + k, node_count)
        return other, (other, local)

    def of_column(k):
        other = lax.rem(column + k, column_count)
        return other, (row * column_count + other, local)

    def of_plane(k):
        me = row * local_count + local
        other = lax.rem(me + k, row_count * local_count)
        return other, (other // local_count * column_count + column, lax.rem(other, local_count))

    local_group = (local_count, local, of_local)
    node_group = (node_count, node, of_node)
    column_group = (column_count, column, of_column)
    plane_group = (row_count * local_count, row * local_count + local, of_plane)

    def each(group, body):
        def step(k, carry):
            body(*group[2](k))
            return carry

        lax.fori_loop(1, group[0], step, 0)

    barrier = pltpu.get_barrier_semaphore()
    for group in (local_group, node_group, plane_group):
        each(group, lambda other, device: pl.semaphore_signal(barrier, inc=1, device_id=device, device_id_type=MESH))

    def exchange(group, source, target, send_sem, recv_sem):
        def send(other, device):
            pltpu.make_async_remote_copy(
                src_ref=source(other), dst_ref=target, send_sem=send_sem, recv_sem=recv_sem,
                device_id=device, device_id_type=MESH,
            ).start()

        each(group, send)
        pltpu.make_async_copy(source(group[1]), target, recv_sem).start()

    def arrived(buffer, recv_sem):
        pltpu.make_async_copy(buffer, buffer, recv_sem).wait()

    loads["ray"].wait()
    rays = ray[...]
    target_node = lax.div(rays, owned * local_count).astype(jnp.float32)
    tile = lax.rem(rays, owned).astype(jnp.float32)
    square = (held, held)
    standing = jnp.sum(
        jnp.where((to_column(target_node) == target_node) & (iota(square, 0) < iota(square, 1)), 1.0, 0.0),
        axis=0,
        keepdims=True,
    )
    position = target_node * SEND_CAPACITY + standing
    spread = (iota((rows_sent, held), 0).astype(jnp.float32) == position).astype(jnp.bfloat16)
    tile_one_hot = (iota((held, LANES), 1).astype(jnp.float32) == to_column(tile)).astype(jnp.bfloat16)
    label_send[...] = dot(spread, tile_one_hot)

    loads["slot"].wait()
    slot_row = jnp.concatenate([slot[...].astype(jnp.float32)] * local_count, axis=1)
    slot_send[...] = jnp.where(iota(slot_row.shape, 1) // block_count == local, slot_row, 0.0)

    loads["direction"].wait()
    loads["pixel"].wait()
    low_direction = direction[...].astype(jnp.bfloat16)
    tile_index = iota((tiles, LANES), 0)
    for c in range(chunks):
        loads["blocks", c].wait()
        chunk_blocks = blocks[pl.ds(c * chunk, chunk)].reshape(chunk * LANES, LANES)
        products = dot(low_direction, chunk_blocks, NT)
        for i in range(chunk):
            b = c * chunk + i
            mine = jnp.where(tile_index == pixel[0, b], products[:, i * LANES : (i + 1) * LANES], 0.0)
            contrib_send[pl.ds(b, 1), :] = jnp.sum(mine, axis=0, keepdims=True)

    pl.semaphore_wait(barrier, local_count + node_count + row_count * local_count - 3)

    my_blocks = pl.ds(pl.multiple_of(local * block_count, block_count), block_count)
    my_rows = pl.ds(node * SEND_CAPACITY, SEND_CAPACITY)

    def rows_of(buffer):
        return lambda other: buffer.at[pl.ds(other * SEND_CAPACITY, SEND_CAPACITY)]

    def blocks_of(buffer):
        return lambda other: buffer.at[pl.ds(pl.multiple_of(other * block_count, block_count), block_count)]

    exchange(local_group, lambda other: contrib_send, contrib_recv.at[my_blocks], y_send_sem.at[1], y_recv_sem.at[1])
    exchange(local_group, lambda other: slot_send, slot_recv.at[local], y_send_sem.at[0], y_recv_sem.at[0])
    exchange(node_group, rows_of(label_send), label_recv.at[my_rows], n_send_sem.at[0], n_recv_sem.at[0])

    arrived(slot_recv, y_recv_sem.at[0])
    group_slot = jnp.sum(slot_recv[...], axis=0) - (local * held).astype(jnp.float32)
    in_slot = (iota((held, group_blocks), 0).astype(jnp.float32) == group_slot).astype(jnp.bfloat16)
    of_slot = (iota((group_blocks, held), 1).astype(jnp.float32) == to_column(group_slot)).astype(jnp.bfloat16)
    gather_rows = dot(spread, in_slot).astype(jnp.bfloat16)
    scatter_rows = dot(of_slot, spread, NT).astype(jnp.bfloat16)

    arrived(contrib_recv, y_recv_sem.at[1])
    held_send[...] = one_hot_dot(gather_rows, contrib_recv[...])
    exchange(node_group, rows_of(held_send), held_recv.at[my_rows], n_send_sem.at[1], n_recv_sem.at[1])

    arrived(label_recv, n_recv_sem.at[0])
    labels = label_recv[...].astype(jnp.bfloat16)
    tile_square = (iota((owned, LANES), 0) == iota((owned, LANES), 1)).astype(jnp.bfloat16)
    collect = dot(tile_square, labels, NT).astype(jnp.bfloat16)
    labels_owned = labels[:, :owned]
    loads["residual"].wait()
    early_send[...] = one_hot_dot(labels_owned, residual[...])
    exchange(node_group, rows_of(early_send), early_recv.at[my_rows], n_send_sem.at[2], n_recv_sem.at[2])

    loads["gradient"].wait()
    loads["image"].wait()
    old_norm_row = jnp.sum(gradient[...] * gradient[...], axis=0, keepdims=True)

    arrived(held_recv, n_recv_sem.at[1])
    projected = one_hot_dot(collect, held_recv[...])
    reply_send[...] = one_hot_dot(labels_owned, projected)
    exchange(node_group, rows_of(reply_send), reply_recv.at[my_rows], n_send_sem.at[3], n_recv_sem.at[3])
    norm_a_send[0:1, :] = jnp.sum(projected * projected, axis=0, keepdims=True)
    norm_a_send[1:2, :] = old_norm_row
    exchange(column_group, lambda other: norm_a_send, norm_a_recv.at[column], s_send_sem.at[0], s_recv_sem.at[0])

    arrived(early_recv, n_recv_sem.at[2])
    early_chosen_send[...] = one_hot_dot(scatter_rows, early_recv[...])
    exchange(
        local_group, blocks_of(early_chosen_send), early_chosen_recv.at[local], y_send_sem.at[2], y_recv_sem.at[2]
    )

    arrived(norm_a_recv, s_recv_sem.at[0])
    norm_b_send[...] = jnp.sum(norm_a_recv[...], axis=0)
    me_in_plane = plane_group[1]
    exchange(plane_group, lambda other: norm_b_send, norm_b_recv.at[me_in_plane], s_send_sem.at[1], s_recv_sem.at[1])

    arrived(reply_recv, n_recv_sem.at[3])
    chosen_send[...] = one_hot_dot(scatter_rows, reply_recv[...])
    exchange(local_group, blocks_of(chosen_send), chosen_recv.at[local], y_send_sem.at[3], y_recv_sem.at[3])

    arrived(norm_b_recv, s_recv_sem.at[1])
    norms = jnp.sum(norm_b_recv[...], axis=0)
    curvature = jnp.sum(norms[0:1, :], axis=1, keepdims=True)
    old_norm = jnp.sum(norms[1:2, :], axis=1, keepdims=True)
    step_size = old_norm / curvature
    image_out[...] = image[...] + step_size * direction[...]
    residual_out[...] = residual[...] - step_size * projected

    arrived(early_chosen_recv, y_recv_sem.at[2])
    old_chosen = jnp.sum(early_chosen_recv[...], axis=0)
    arrived(chosen_recv, y_recv_sem.at[3])
    chosen = old_chosen - step_size * jnp.sum(chosen_recv[...], axis=0)

    gradient_new = jnp.zeros((tiles, LANES), jnp.float32)
    for c in range(chunks):
        spread_residual = jnp.concatenate(
            [
                jnp.where(tile_index == pixel[0, b], chosen[b : b + 1, :], 0.0)
                for b in range(c * chunk, (c + 1) * chunk)
            ],
            axis=1,
        ).astype(jnp.bfloat16)
        chunk_blocks = blocks[pl.ds(c * chunk, chunk)].reshape(chunk * LANES, LANES)
        gradient_new += dot(spread_residual, chunk_blocks)

    last_a_send[...] = jnp.sum(gradient_new * gradient_new, axis=0, keepdims=True)
    exchange(column_group, lambda other: last_a_send, last_a_recv.at[column], s_send_sem.at[2], s_recv_sem.at[2])
    arrived(last_a_recv, s_recv_sem.at[2])
    last_b_send[...] = jnp.sum(last_a_recv[...], axis=0)
    exchange(plane_group, lambda other: last_b_send, last_b_recv.at[me_in_plane], s_send_sem.at[3], s_recv_sem.at[3])
    arrived(last_b_recv, s_recv_sem.at[3])
    new_norm = jnp.sum(jnp.sum(last_b_recv[...], axis=0), axis=1, keepdims=True)
    direction_out[...] = gradient_new + (new_norm / old_norm) * direction[...]

    def sent(group, buffer, each_rows, send_sem):
        sample = buffer.at[pl.ds(0, (group[0] - 1) * each_rows)]
        pltpu.make_async_copy(sample, sample, send_sem).wait()

    sent(local_group, slot_recv, 1, y_send_sem.at[0])
    sent(local_group, contrib_recv, block_count, y_send_sem.at[1])
    sent(local_group, early_chosen_recv, 1, y_send_sem.at[2])
    sent(local_group, chosen_recv, 1, y_send_sem.at[3])
    for index, buffer in enumerate((label_recv, held_recv, early_recv, reply_recv)):
        sent(node_group, buffer, SEND_CAPACITY, n_send_sem.at[index])
    sent(column_group, norm_a_recv, 1, s_send_sem.at[0])
    sent(plane_group, norm_b_recv, 1, s_send_sem.at[1])
    sent(column_group, last_a_recv, 1, s_send_sem.at[2])
    sent(plane_group, last_b_recv, 1, s_send_sem.at[3])


def solution(mesh):
    node_count, local_count = mesh.shape["node"], mesh.shape["local"]
    row_count = 4 if node_count % 4 == 0 and node_count > 4 else 2
    column_count = node_count // row_count
    plane_count = row_count * local_count

    def on_device(image, direction, gradient, residual, blocks, block_slot, block_pixel, slot_ray):
        rows_sent = node_count * SEND_CAPACITY
        block_count, held = block_slot.shape[0], slot_ray.shape[0]
        group_blocks = block_count * local_count
        chosen_shape = (local_count, block_count, LANES)

        def f32(*shape):
            return pltpu.VMEM(shape, jnp.float32)

        def pair(send, recv):
            return [f32(*send), f32(*recv)]

        rows, group = (rows_sent, LANES), (group_blocks, LANES)
        scratch = [
            f32(*image.shape), f32(*image.shape), f32(*image.shape), f32(*residual.shape),
            pltpu.VMEM(blocks.shape, jnp.bfloat16), pltpu.VMEM((1, block_count), jnp.int32),
            pltpu.SMEM((1, block_count), jnp.int32), pltpu.VMEM((1, held), jnp.int32),
            pltpu.SemaphoreType.DMA((11,)),
            *pair((1, group_blocks), (local_count, 1, group_blocks)),
            *pair(rows, rows),
            *pair((block_count, LANES), group),
            *pair(rows, rows),
            *pair(rows, rows),
            *pair(group, chosen_shape),
            *pair(rows, rows),
            *pair(group, chosen_shape),
            *pair((2, LANES), (column_count, 2, LANES)),
            *pair((2, LANES), (plane_count, 2, LANES)),
            *pair((1, LANES), (column_count, 1, LANES)),
            *pair((1, LANES), (plane_count, 1, LANES)),
            *[pltpu.SemaphoreType.DMA((4,))] * 6,
        ]
        return pl.pallas_call(
            functools.partial(kernel, (node_count, local_count, row_count)),
            out_shape=tuple(jax.ShapeDtypeStruct(a.shape, jnp.float32) for a in (image, residual, direction)),
            in_specs=[pl.BlockSpec(memory_space=pl.ANY)] * 8,
            out_specs=[pl.BlockSpec(memory_space=pltpu.VMEM)] * 3,
            scratch_shapes=scratch,
            compiler_params=pltpu.CompilerParams(
                collective_id=0, has_side_effects=True, vmem_limit_bytes=32 * 1024 * 1024
            ),
        )(
            image, direction, gradient, residual, blocks,
            block_slot.reshape(1, block_count), block_pixel.reshape(1, block_count), slot_ray.reshape(1, held),
        )

    split = P(("node", "local"))
    return jax.shard_map(
        on_device,
        mesh=mesh,
        in_specs=(split,) * 8,
        out_specs=(split,) * 3,
        check_vma=False,
    )
```

```python
import functools

import jax
import jax.numpy as jnp
from jax import lax
from jax.experimental import pallas as pl
from jax.experimental.pallas import tpu as pltpu
from jax.sharding import PartitionSpec as P

SEND_CAPACITY = 2
LANES = 128
MESH = pl.DeviceIdType.MESH
NT = (((1,), (1,)), ((), ()))


def iota(shape, axis):
    return lax.broadcasted_iota(jnp.int32, shape, axis)


def dot(a, b, dims=(((1,), (0,)), ((), ()))):
    return lax.dot_general(a, b, dims, preferred_element_type=jnp.float32)


def one_hot_dot(one_hot, value):
    high = value.astype(jnp.bfloat16)
    rest = value - high.astype(jnp.float32)
    middle = rest.astype(jnp.bfloat16)
    low = (rest - middle.astype(jnp.float32)).astype(jnp.bfloat16)
    width = value.shape[1]
    out = dot(one_hot, jnp.concatenate([high, middle, low], axis=1))
    return out[:, :width] + (out[:, width : 2 * width] + out[:, 2 * width :])


def to_column(row):
    length = row.shape[1]
    square = (length, length)
    return jnp.sum(jnp.where(iota(square, 0) == iota(square, 1), row, 0.0), axis=1, keepdims=True)


def kernel(
    sizes,
    image_hbm, direction_hbm, gradient_hbm, residual_hbm, blocks_hbm, slot_hbm, pixel_hbm, ray_hbm,
    image_out, residual_out, direction_out,
    image, direction, gradient, residual, blocks, slot, pixel, ray, load_sem,
    slot_send, slot_recv, label_send, label_recv,
    contrib_send, contrib_recv, held_send, held_recv,
    reply_send, reply_recv, chosen_send, chosen_recv,
    early_send, early_recv, early_chosen_send, early_chosen_recv,
    norm_a_send, norm_a_recv, norm_b_send, norm_b_recv,
    last_a_send, last_a_recv, last_b_send, last_b_recv,
    y_send_sem, y_recv_sem, n_send_sem, n_recv_sem, s_send_sem, s_recv_sem, round_sem,
):
    node_count, local_count, x_count = sizes
    z_count = node_count // (2 * x_count)
    node = lax.axis_index("node")
    local = lax.axis_index("local")
    x = node // (2 * z_count)
    z = lax.rem(node, 2 * z_count) // 2
    core = lax.rem(node, 2)
    tiles, block_count = image.shape[0], blocks.shape[0]
    held, owned = ray.shape[1], residual.shape[0]
    rows_sent = node_count * SEND_CAPACITY
    group_blocks = block_count * local_count

    chunks = 4
    chunk = block_count // chunks
    loads = {}
    for index, (name, source, target) in enumerate(
        (
            ("ray", ray_hbm, ray),
            ("direction", direction_hbm, direction),
            ("pixel", pixel_hbm, pixel),
            ("slot", slot_hbm, slot),
            *(
                (("blocks", c), blocks_hbm.at[pl.ds(c * chunk, chunk)], blocks.at[pl.ds(c * chunk, chunk)])
                for c in range(chunks)
            ),
            ("gradient", gradient_hbm, gradient),
            ("residual", residual_hbm, residual),
            ("image", image_hbm, image),
        )
    ):
        loads[name] = pltpu.make_async_copy(source, target, load_sem.at[index])
        loads[name].start()

    def ring(place, size):
        def at(i):
            shift = size // 2 + (i // 2 if i % 2 == 0 else -((i + 1) // 2))
            return place + shift - jnp.where(place + shift >= size, size, 0)

        return [at(i) for i in range(size)]

    x_ring, core_ring, local_ring = ring(x, x_count), ring(core, 2), ring(local, local_count)

    def z_at(i):
        shift = z_count // 2 + jnp.where(lax.rem(i, 2) == 0, i // 2, -((i + 1) // 2))
        return z + shift - jnp.where(z + shift >= z_count, z_count, 0)

    def node_of(x, z, core):
        return (x * z_count + z) * 2 + core

    def along_z(others, body):
        def step(i, carry):
            for other_x, other_core in others:
                body(other_x, z_at(i), other_core)
            return carry

        lax.fori_loop(0, z_count - 1, step, 0)
        for other_x, other_core in others[:-1]:
            body(other_x, z, other_core)

    def of_local(body):
        for other in local_ring[:-1]:
            body(other, (node, other))

    def of_xc(body):
        for other_x, other_core in [(a, b) for a in x_ring for b in core_ring][:-1]:
            body(other_x * 2 + other_core, (node_of(other_x, z, other_core), local))

    def of_z(body):
        along_z([(x, core)], lambda x, z, core: body(z, (node_of(x, z, core), local)))

    def of_node(body):
        def member(x, z, core):
            other = node_of(x, z, core)
            body(other, (other, local))

        along_z([(a, b) for a in x_ring for b in core_ring], member)

    def of_column(body):
        along_z([(x, b) for b in core_ring], lambda x, z, core: body(z * 2 + core, (node_of(x, z, core), local)))

    def of_plane(body):
        for other_local, other_x in [(a, b) for a in local_ring for b in x_ring][:-1]:
            body(other_x * local_count + other_local, (node_of(other_x, z, core), other_local))

    local_group = (local_count, local, of_local)
    node_group = (node_count, node, of_node)
    column_group = (z_count * 2, z * 2 + core, of_column)
    plane_group = (x_count * local_count, x * local_count + local, of_plane)

    barrier = pltpu.get_barrier_semaphore()

    def greet(semaphore):
        return lambda other, device: pl.semaphore_signal(semaphore, inc=1, device_id=device, device_id_type=MESH)

    of_local(greet(barrier))
    of_xc(greet(barrier))
    of_z(greet(barrier))

    def exchange(group, source, target, send_sem, recv_sem):
        def send(other, device):
            pltpu.make_async_remote_copy(
                src_ref=source(other), dst_ref=target, send_sem=send_sem, recv_sem=recv_sem,
                device_id=device, device_id_type=MESH,
            ).start()

        group[2](send)
        pltpu.make_async_copy(source(group[1]), target, recv_sem).start()

    def arrived(buffer, recv_sem):
        pltpu.make_async_copy(buffer, buffer, recv_sem).wait()

    loads["ray"].wait()
    rays = ray[...]
    target_node = lax.div(rays, owned * local_count).astype(jnp.float32)
    tile = lax.rem(rays, owned).astype(jnp.float32)
    square = (held, held)
    standing = jnp.sum(
        jnp.where((to_column(target_node) == target_node) & (iota(square, 0) < iota(square, 1)), 1.0, 0.0),
        axis=0,
        keepdims=True,
    )
    position = target_node * SEND_CAPACITY + standing
    spread = (iota((rows_sent, held), 0).astype(jnp.float32) == position).astype(jnp.bfloat16)
    tile_one_hot = (iota((held, LANES), 1).astype(jnp.float32) == to_column(tile)).astype(jnp.bfloat16)
    label_send[...] = dot(spread, tile_one_hot)

    loads["slot"].wait()
    slot_row = jnp.concatenate([slot[...].astype(jnp.float32)] * local_count, axis=1)
    slot_send[...] = jnp.where(iota(slot_row.shape, 1) // block_count == local, slot_row, 0.0)

    loads["direction"].wait()
    loads["pixel"].wait()
    low_direction = direction[...].astype(jnp.bfloat16)
    tile_index = iota((tiles, LANES), 0)
    for c in range(chunks):
        loads["blocks", c].wait()
        chunk_blocks = blocks[pl.ds(c * chunk, chunk)].reshape(chunk * LANES, LANES)
        products = dot(low_direction, chunk_blocks, NT)
        for i in range(chunk):
            b = c * chunk + i
            mine = jnp.where(tile_index == pixel[0, b], products[:, i * LANES : (i + 1) * LANES], 0.0)
            contrib_send[pl.ds(b, 1), :] = jnp.sum(mine, axis=0, keepdims=True)

    pl.semaphore_wait(barrier, local_count + z_count + 2 * x_count - 3)

    my_blocks = pl.ds(pl.multiple_of(local * block_count, block_count), block_count)
    my_rows = pl.ds(node * SEND_CAPACITY, SEND_CAPACITY)

    def rows_of(buffer):
        return lambda other: buffer.at[pl.ds(other * SEND_CAPACITY, SEND_CAPACITY)]

    def blocks_of(buffer):
        return lambda other: buffer.at[pl.ds(pl.multiple_of(other * block_count, block_count), block_count)]

    exchange(local_group, lambda other: contrib_send, contrib_recv.at[my_blocks], y_send_sem.at[1], y_recv_sem.at[1])
    exchange(local_group, lambda other: slot_send, slot_recv.at[local], y_send_sem.at[0], y_recv_sem.at[0])
    of_z(greet(round_sem.at[0]))
    of_local(greet(round_sem.at[1]))
    pl.semaphore_wait(round_sem.at[0], z_count - 1)
    exchange(node_group, rows_of(label_send), label_recv.at[my_rows], n_send_sem.at[0], n_recv_sem.at[0])

    arrived(slot_recv, y_recv_sem.at[0])
    group_slot = jnp.sum(slot_recv[...], axis=0) - (local * held).astype(jnp.float32)
    in_slot = (iota((held, group_blocks), 0).astype(jnp.float32) == group_slot).astype(jnp.bfloat16)
    of_slot = (iota((group_blocks, held), 1).astype(jnp.float32) == to_column(group_slot)).astype(jnp.bfloat16)
    gather_rows = dot(spread, in_slot).astype(jnp.bfloat16)
    scatter_rows = dot(of_slot, spread, NT).astype(jnp.bfloat16)

    arrived(contrib_recv, y_recv_sem.at[1])
    held_send[...] = one_hot_dot(gather_rows, contrib_recv[...])
    exchange(node_group, rows_of(held_send), held_recv.at[my_rows], n_send_sem.at[1], n_recv_sem.at[1])

    arrived(label_recv, n_recv_sem.at[0])
    labels = label_recv[...].astype(jnp.bfloat16)
    tile_square = (iota((owned, LANES), 0) == iota((owned, LANES), 1)).astype(jnp.bfloat16)
    collect = dot(tile_square, labels, NT).astype(jnp.bfloat16)
    labels_owned = labels[:, :owned]
    loads["residual"].wait()
    early_send[...] = one_hot_dot(labels_owned, residual[...])
    exchange(node_group, rows_of(early_send), early_recv.at[my_rows], n_send_sem.at[2], n_recv_sem.at[2])

    loads["gradient"].wait()
    loads["image"].wait()
    old_norm_row = jnp.sum(gradient[...] * gradient[...], axis=0, keepdims=True)

    arrived(held_recv, n_recv_sem.at[1])
    projected = one_hot_dot(collect, held_recv[...])
    reply_send[...] = one_hot_dot(labels_owned, projected)
    exchange(node_group, rows_of(reply_send), reply_recv.at[my_rows], n_send_sem.at[3], n_recv_sem.at[3])
    norm_a_send[0:1, :] = jnp.sum(projected * projected, axis=0, keepdims=True)
    norm_a_send[1:2, :] = old_norm_row
    exchange(column_group, lambda other: norm_a_send, norm_a_recv.at[column_group[1]], s_send_sem.at[0], s_recv_sem.at[0])

    arrived(early_recv, n_recv_sem.at[2])
    early_chosen_send[...] = one_hot_dot(scatter_rows, early_recv[...])
    exchange(
        local_group, blocks_of(early_chosen_send), early_chosen_recv.at[local], y_send_sem.at[2], y_recv_sem.at[2]
    )

    arrived(norm_a_recv, s_recv_sem.at[0])
    norm_b_send[...] = jnp.sum(norm_a_recv[...], axis=0)
    me_in_plane = plane_group[1]
    pl.semaphore_wait(round_sem.at[1], local_count - 1)
    exchange(plane_group, lambda other: norm_b_send, norm_b_recv.at[me_in_plane], s_send_sem.at[1], s_recv_sem.at[1])

    arrived(reply_recv, n_recv_sem.at[3])
    chosen_send[...] = one_hot_dot(scatter_rows, reply_recv[...])
    exchange(local_group, blocks_of(chosen_send), chosen_recv.at[local], y_send_sem.at[3], y_recv_sem.at[3])

    arrived(norm_b_recv, s_recv_sem.at[1])
    norms = jnp.sum(norm_b_recv[...], axis=0)
    curvature = jnp.sum(norms[0:1, :], axis=1, keepdims=True)
    old_norm = jnp.sum(norms[1:2, :], axis=1, keepdims=True)
    step_size = old_norm / curvature
    image_out[...] = image[...] + step_size * direction[...]
    residual_out[...] = residual[...] - step_size * projected

    arrived(early_chosen_recv, y_recv_sem.at[2])
    old_chosen = jnp.sum(early_chosen_recv[...], axis=0)
    arrived(chosen_recv, y_recv_sem.at[3])
    chosen = old_chosen - step_size * jnp.sum(chosen_recv[...], axis=0)

    gradient_new = jnp.zeros((tiles, LANES), jnp.float32)
    for c in range(chunks):
        spread_residual = jnp.concatenate(
            [
                jnp.where(tile_index == pixel[0, b], chosen[b : b + 1, :], 0.0)
                for b in range(c * chunk, (c + 1) * chunk)
            ],
            axis=1,
        ).astype(jnp.bfloat16)
        chunk_blocks = blocks[pl.ds(c * chunk, chunk)].reshape(chunk * LANES, LANES)
        gradient_new += dot(spread_residual, chunk_blocks)

    last_a_send[...] = jnp.sum(gradient_new * gradient_new, axis=0, keepdims=True)
    exchange(column_group, lambda other: last_a_send, last_a_recv.at[column_group[1]], s_send_sem.at[2], s_recv_sem.at[2])
    arrived(last_a_recv, s_recv_sem.at[2])
    last_b_send[...] = jnp.sum(last_a_recv[...], axis=0)
    exchange(plane_group, lambda other: last_b_send, last_b_recv.at[me_in_plane], s_send_sem.at[3], s_recv_sem.at[3])
    arrived(last_b_recv, s_recv_sem.at[3])
    new_norm = jnp.sum(jnp.sum(last_b_recv[...], axis=0), axis=1, keepdims=True)
    direction_out[...] = gradient_new + (new_norm / old_norm) * direction[...]

    def sent(group, buffer, each_rows, send_sem):
        sample = buffer.at[pl.ds(0, (group[0] - 1) * each_rows)]
        pltpu.make_async_copy(sample, sample, send_sem).wait()

    sent(local_group, slot_recv, 1, y_send_sem.at[0])
    sent(local_group, contrib_recv, block_count, y_send_sem.at[1])
    sent(local_group, early_chosen_recv, 1, y_send_sem.at[2])
    sent(local_group, chosen_recv, 1, y_send_sem.at[3])
    for index, buffer in enumerate((label_recv, held_recv, early_recv, reply_recv)):
        sent(node_group, buffer, SEND_CAPACITY, n_send_sem.at[index])
    sent(column_group, norm_a_recv, 1, s_send_sem.at[0])
    sent(plane_group, norm_b_recv, 1, s_send_sem.at[1])
    sent(column_group, last_a_recv, 1, s_send_sem.at[2])
    sent(plane_group, last_b_recv, 1, s_send_sem.at[3])


def solution(mesh):
    node_count, local_count = mesh.shape["node"], mesh.shape["local"]
    x_count = 4 if node_count % 16 == 0 else 2
    column_count = node_count // x_count
    plane_count = x_count * local_count

    def on_device(image, direction, gradient, residual, blocks, block_slot, block_pixel, slot_ray):
        rows_sent = node_count * SEND_CAPACITY
        block_count, held = block_slot.shape[0], slot_ray.shape[0]
        group_blocks = block_count * local_count
        chosen_shape = (local_count, block_count, LANES)

        def f32(*shape):
            return pltpu.VMEM(shape, jnp.float32)

        def pair(send, recv):
            return [f32(*send), f32(*recv)]

        rows, group = (rows_sent, LANES), (group_blocks, LANES)
        scratch = [
            f32(*image.shape), f32(*image.shape), f32(*image.shape), f32(*residual.shape),
            pltpu.VMEM(blocks.shape, jnp.bfloat16), pltpu.VMEM((1, block_count), jnp.int32),
            pltpu.SMEM((1, block_count), jnp.int32), pltpu.VMEM((1, held), jnp.int32),
            pltpu.SemaphoreType.DMA((11,)),
            *pair((1, group_blocks), (local_count, 1, group_blocks)),
            *pair(rows, rows),
            *pair((block_count, LANES), group),
            *pair(rows, rows),
            *pair(rows, rows),
            *pair(group, chosen_shape),
            *pair(rows, rows),
            *pair(group, chosen_shape),
            *pair((2, LANES), (column_count, 2, LANES)),
            *pair((2, LANES), (plane_count, 2, LANES)),
            *pair((1, LANES), (column_count, 1, LANES)),
            *pair((1, LANES), (plane_count, 1, LANES)),
            *[pltpu.SemaphoreType.DMA((4,))] * 6, pltpu.SemaphoreType.REGULAR((2,)),
        ]
        return pl.pallas_call(
            functools.partial(kernel, (node_count, local_count, x_count)),
            out_shape=tuple(jax.ShapeDtypeStruct(a.shape, jnp.float32) for a in (image, residual, direction)),
            in_specs=[pl.BlockSpec(memory_space=pltpu.HBM)] * 8,
            out_specs=[pl.BlockSpec(memory_space=pltpu.VMEM)] * 3,
            scratch_shapes=scratch,
            compiler_params=pltpu.CompilerParams(
                collective_id=0, has_side_effects=True, vmem_limit_bytes=60 * 1024 * 1024
            ),
        )(
            image, direction, gradient, residual, blocks,
            block_slot.reshape(1, block_count), block_pixel.reshape(1, block_count), slot_ray.reshape(1, held),
        )

    split = P(("node", "local"))
    return jax.shard_map(
        on_device,
        mesh=mesh,
        in_specs=(split,) * 8,
        out_specs=(split,) * 3,
        check_vma=False,
    )
```

```python
import functools

import jax
import jax.numpy as jnp
from jax import lax
from jax.experimental import pallas as pl
from jax.experimental.pallas import tpu as pltpu
from jax.sharding import PartitionSpec as P

SEND_CAPACITY = 2
LANES = 128
MESH = pl.DeviceIdType.MESH
NT = (((1,), (1,)), ((), ()))


def iota(shape, axis):
    return lax.broadcasted_iota(jnp.int32, shape, axis)


def dot(a, b, dims=(((1,), (0,)), ((), ()))):
    return lax.dot_general(a, b, dims, preferred_element_type=jnp.float32)


def one_hot_dot(one_hot, value):
    high = value.astype(jnp.bfloat16)
    rest = value - high.astype(jnp.float32)
    middle = rest.astype(jnp.bfloat16)
    low = (rest - middle.astype(jnp.float32)).astype(jnp.bfloat16)
    width = value.shape[1]
    out = dot(one_hot, jnp.concatenate([high, middle, low], axis=1))
    return out[:, :width] + (out[:, width : 2 * width] + out[:, 2 * width :])


def to_column(row):
    length = row.shape[1]
    square = (length, length)
    return jnp.sum(jnp.where(iota(square, 0) == iota(square, 1), row, 0.0), axis=1, keepdims=True)


def kernel(
    sizes,
    image_hbm, direction_hbm, gradient_hbm, residual_hbm, blocks_hbm, slot_hbm, pixel_hbm, ray_hbm,
    image_out, residual_out, direction_out,
    image, direction, gradient, residual, blocks, slot, pixel, ray, load_sem,
    slot_send, slot_recv, label_send, label_recv,
    contrib_send, contrib_recv, held_send, held_recv,
    reply_send, reply_recv, chosen_send, chosen_recv,
    early_send, early_recv, early_chosen_send, early_chosen_recv,
    norm_a_send, norm_a_recv, norm_b_send, norm_b_recv,
    last_a_send, last_a_recv, last_b_send, last_b_recv,
    y_send_sem, y_recv_sem, n_send_sem, n_recv_sem, s_send_sem, s_recv_sem, round_sem,
):
    node_count, local_count, x_count = sizes
    z_count = node_count // (2 * x_count)
    node = lax.axis_index("node")
    local = lax.axis_index("local")
    x = node // (2 * z_count)
    z = lax.rem(node, 2 * z_count) // 2
    core = lax.rem(node, 2)
    tiles, block_count = image.shape[0], blocks.shape[0]
    held, owned = ray.shape[1], residual.shape[0]
    rows_sent = node_count * SEND_CAPACITY
    group_blocks = block_count * local_count

    def ring(place, size):
        def at(i):
            shift = size // 2 + (i // 2 if i % 2 == 0 else -((i + 1) // 2))
            return place + shift - jnp.where(place + shift >= size, size, 0)

        return [at(i) for i in range(size)]

    x_ring, core_ring, local_ring = ring(x, x_count), ring(core, 2), ring(local, local_count)

    def z_at(i):
        shift = z_count // 2 + jnp.where(lax.rem(i, 2) == 0, i // 2, -((i + 1) // 2))
        return z + shift - jnp.where(z + shift >= z_count, z_count, 0)

    def node_of(x, z, core):
        return (x * z_count + z) * 2 + core

    def along_z(others, body):
        def step(i, carry):
            for other_x, other_core in others:
                body(other_x, z_at(i), other_core)
            return carry

        lax.fori_loop(0, z_count - 1, step, 0)
        for other_x, other_core in others[:-1]:
            body(other_x, z, other_core)

    def of_local(body):
        for other in local_ring[:-1]:
            body(other, (node, other))

    def of_xc(body):
        for other_x, other_core in [(a, b) for a in x_ring for b in core_ring][:-1]:
            body(other_x * 2 + other_core, (node_of(other_x, z, other_core), local))

    def of_z(body):
        along_z([(x, core)], lambda x, z, core: body(z, (node_of(x, z, core), local)))

    def of_node(body):
        def member(x, z, core):
            other = node_of(x, z, core)
            body(other, (other, local))

        along_z([(a, b) for a in x_ring for b in core_ring], member)

    def of_column(body):
        along_z([(x, b) for b in core_ring], lambda x, z, core: body(z * 2 + core, (node_of(x, z, core), local)))

    def of_plane(body):
        for other_local, other_x in [(a, b) for a in local_ring for b in x_ring][:-1]:
            body(other_x * local_count + other_local, (node_of(other_x, z, core), other_local))

    local_group = (local_count, local, of_local)
    node_group = (node_count, node, of_node)
    column_group = (z_count * 2, z * 2 + core, of_column)
    plane_group = (x_count * local_count, x * local_count + local, of_plane)

    barrier = pltpu.get_barrier_semaphore()

    def greet(semaphore):
        return lambda other, device: pl.semaphore_signal(semaphore, inc=1, device_id=device, device_id_type=MESH)

    of_z(greet(barrier))
    of_xc(greet(barrier))
    of_local(greet(barrier))

    chunks = 4
    chunk = block_count // chunks
    loads = {}
    for index, (name, source, target) in enumerate(
        (
            ("ray", ray_hbm, ray),
            ("direction", direction_hbm, direction),
            ("pixel", pixel_hbm, pixel),
            ("slot", slot_hbm, slot),
            *(
                (("blocks", c), blocks_hbm.at[pl.ds(c * chunk, chunk)], blocks.at[pl.ds(c * chunk, chunk)])
                for c in range(chunks)
            ),
            ("gradient", gradient_hbm, gradient),
            ("residual", residual_hbm, residual),
            ("image", image_hbm, image),
        )
    ):
        loads[name] = pltpu.make_async_copy(source, target, load_sem.at[index])
        loads[name].start()

    def exchange(group, source, target, send_sem, recv_sem):
        def send(other, device):
            pltpu.make_async_remote_copy(
                src_ref=source(other), dst_ref=target, send_sem=send_sem, recv_sem=recv_sem,
                device_id=device, device_id_type=MESH,
            ).start()

        group[2](send)
        pltpu.make_async_copy(source(group[1]), target, recv_sem).start()

    def arrived(buffer, recv_sem):
        pltpu.make_async_copy(buffer, buffer, recv_sem).wait()

    loads["ray"].wait()
    rays = ray[...]
    target_node = lax.div(rays, owned * local_count).astype(jnp.float32)
    tile = lax.rem(rays, owned).astype(jnp.float32)
    square = (held, held)
    standing = jnp.sum(
        jnp.where((to_column(target_node) == target_node) & (iota(square, 0) < iota(square, 1)), 1.0, 0.0),
        axis=0,
        keepdims=True,
    )
    position = target_node * SEND_CAPACITY + standing
    spread = (iota((rows_sent, held), 0).astype(jnp.float32) == position).astype(jnp.bfloat16)
    tile_one_hot = (iota((held, LANES), 1).astype(jnp.float32) == to_column(tile)).astype(jnp.bfloat16)
    label_send[...] = dot(spread, tile_one_hot)

    loads["slot"].wait()
    slot_row = jnp.concatenate([slot[...].astype(jnp.float32)] * local_count, axis=1)
    slot_send[...] = jnp.where(iota(slot_row.shape, 1) // block_count == local, slot_row, 0.0)

    loads["direction"].wait()
    loads["pixel"].wait()
    low_direction = direction[...].astype(jnp.bfloat16)
    tile_index = iota((tiles, LANES), 0)
    for c in range(chunks):
        loads["blocks", c].wait()
        chunk_blocks = blocks[pl.ds(c * chunk, chunk)].reshape(chunk * LANES, LANES)
        products = dot(low_direction, chunk_blocks, NT)
        for i in range(chunk):
            b = c * chunk + i
            mine = jnp.where(tile_index == pixel[0, b], products[:, i * LANES : (i + 1) * LANES], 0.0)
            contrib_send[pl.ds(b, 1), :] = jnp.sum(mine, axis=0, keepdims=True)

    pl.semaphore_wait(barrier, local_count + z_count + 2 * x_count - 3)

    my_blocks = pl.ds(pl.multiple_of(local * block_count, block_count), block_count)
    my_rows = pl.ds(node * SEND_CAPACITY, SEND_CAPACITY)

    def rows_of(buffer):
        return lambda other: buffer.at[pl.ds(other * SEND_CAPACITY, SEND_CAPACITY)]

    def blocks_of(buffer):
        return lambda other: buffer.at[pl.ds(pl.multiple_of(other * block_count, block_count), block_count)]

    exchange(local_group, lambda other: contrib_send, contrib_recv.at[my_blocks], y_send_sem.at[1], y_recv_sem.at[1])
    exchange(local_group, lambda other: slot_send, slot_recv.at[local], y_send_sem.at[0], y_recv_sem.at[0])
    of_z(greet(round_sem.at[0]))
    of_local(greet(round_sem.at[1]))
    pl.semaphore_wait(round_sem.at[0], z_count - 1)
    exchange(node_group, rows_of(label_send), label_recv.at[my_rows], n_send_sem.at[0], n_recv_sem.at[0])

    arrived(slot_recv, y_recv_sem.at[0])
    group_slot = jnp.sum(slot_recv[...], axis=0) - (local * held).astype(jnp.float32)
    in_slot = (iota((held, group_blocks), 0).astype(jnp.float32) == group_slot).astype(jnp.bfloat16)
    of_slot = (iota((group_blocks, held), 1).astype(jnp.float32) == to_column(group_slot)).astype(jnp.bfloat16)
    gather_rows = dot(spread, in_slot).astype(jnp.bfloat16)
    scatter_rows = dot(of_slot, spread, NT).astype(jnp.bfloat16)

    arrived(contrib_recv, y_recv_sem.at[1])
    held_send[...] = one_hot_dot(gather_rows, contrib_recv[...])
    exchange(node_group, rows_of(held_send), held_recv.at[my_rows], n_send_sem.at[1], n_recv_sem.at[1])

    arrived(label_recv, n_recv_sem.at[0])
    labels = label_recv[...].astype(jnp.bfloat16)
    tile_square = (iota((owned, LANES), 0) == iota((owned, LANES), 1)).astype(jnp.bfloat16)
    collect = dot(tile_square, labels, NT).astype(jnp.bfloat16)
    labels_owned = labels[:, :owned]
    loads["residual"].wait()
    early_send[...] = one_hot_dot(labels_owned, residual[...])
    exchange(node_group, rows_of(early_send), early_recv.at[my_rows], n_send_sem.at[2], n_recv_sem.at[2])

    loads["gradient"].wait()
    loads["image"].wait()
    old_norm_row = jnp.sum(gradient[...] * gradient[...], axis=0, keepdims=True)

    arrived(held_recv, n_recv_sem.at[1])
    projected = one_hot_dot(collect, held_recv[...])
    reply_send[...] = one_hot_dot(labels_owned, projected)
    exchange(node_group, rows_of(reply_send), reply_recv.at[my_rows], n_send_sem.at[3], n_recv_sem.at[3])
    norm_a_send[0:1, :] = jnp.sum(projected * projected, axis=0, keepdims=True)
    norm_a_send[1:2, :] = old_norm_row
    exchange(column_group, lambda other: norm_a_send, norm_a_recv.at[column_group[1]], s_send_sem.at[0], s_recv_sem.at[0])

    arrived(early_recv, n_recv_sem.at[2])
    early_chosen_send[...] = one_hot_dot(scatter_rows, early_recv[...])
    exchange(
        local_group, blocks_of(early_chosen_send), early_chosen_recv.at[local], y_send_sem.at[2], y_recv_sem.at[2]
    )

    arrived(norm_a_recv, s_recv_sem.at[0])
    norm_b_send[...] = jnp.sum(norm_a_recv[...], axis=0)
    me_in_plane = plane_group[1]
    pl.semaphore_wait(round_sem.at[1], local_count - 1)
    exchange(plane_group, lambda other: norm_b_send, norm_b_recv.at[me_in_plane], s_send_sem.at[1], s_recv_sem.at[1])

    arrived(reply_recv, n_recv_sem.at[3])
    chosen_send[...] = one_hot_dot(scatter_rows, reply_recv[...])
    exchange(local_group, blocks_of(chosen_send), chosen_recv.at[local], y_send_sem.at[3], y_recv_sem.at[3])

    arrived(norm_b_recv, s_recv_sem.at[1])
    norms = jnp.sum(norm_b_recv[...], axis=0)
    curvature = jnp.sum(norms[0:1, :], axis=1, keepdims=True)
    old_norm = jnp.sum(norms[1:2, :], axis=1, keepdims=True)
    step_size = old_norm / curvature
    image_out[...] = image[...] + step_size * direction[...]
    residual_out[...] = residual[...] - step_size * projected

    arrived(early_chosen_recv, y_recv_sem.at[2])
    old_chosen = jnp.sum(early_chosen_recv[...], axis=0)
    arrived(chosen_recv, y_recv_sem.at[3])
    chosen = old_chosen - step_size * jnp.sum(chosen_recv[...], axis=0)

    gradient_new = jnp.zeros((tiles, LANES), jnp.float32)
    for c in range(chunks):
        spread_residual = jnp.concatenate(
            [
                jnp.where(tile_index == pixel[0, b], chosen[b : b + 1, :], 0.0)
                for b in range(c * chunk, (c + 1) * chunk)
            ],
            axis=1,
        ).astype(jnp.bfloat16)
        chunk_blocks = blocks[pl.ds(c * chunk, chunk)].reshape(chunk * LANES, LANES)
        gradient_new += dot(spread_residual, chunk_blocks)

    last_a_send[...] = jnp.sum(gradient_new * gradient_new, axis=0, keepdims=True)
    exchange(column_group, lambda other: last_a_send, last_a_recv.at[column_group[1]], s_send_sem.at[2], s_recv_sem.at[2])
    arrived(last_a_recv, s_recv_sem.at[2])
    last_b_send[...] = jnp.sum(last_a_recv[...], axis=0)
    exchange(plane_group, lambda other: last_b_send, last_b_recv.at[me_in_plane], s_send_sem.at[3], s_recv_sem.at[3])
    arrived(last_b_recv, s_recv_sem.at[3])
    new_norm = jnp.sum(jnp.sum(last_b_recv[...], axis=0), axis=1, keepdims=True)
    direction_out[...] = gradient_new + (new_norm / old_norm) * direction[...]

    def sent(group, buffer, each_rows, send_sem):
        sample = buffer.at[pl.ds(0, (group[0] - 1) * each_rows)]
        pltpu.make_async_copy(sample, sample, send_sem).wait()

    sent(local_group, slot_recv, 1, y_send_sem.at[0])
    sent(local_group, contrib_recv, block_count, y_send_sem.at[1])
    sent(local_group, early_chosen_recv, 1, y_send_sem.at[2])
    sent(local_group, chosen_recv, 1, y_send_sem.at[3])
    for index, buffer in enumerate((label_recv, held_recv, early_recv, reply_recv)):
        sent(node_group, buffer, SEND_CAPACITY, n_send_sem.at[index])
    sent(column_group, norm_a_recv, 1, s_send_sem.at[0])
    sent(plane_group, norm_b_recv, 1, s_send_sem.at[1])
    sent(column_group, last_a_recv, 1, s_send_sem.at[2])
    sent(plane_group, last_b_recv, 1, s_send_sem.at[3])


def hand_on(*refs):
    arrays = len(refs) // 2
    for i in range(arrays):
        refs[arrays + i][...] = refs[i][...]


def solution(mesh):
    node_count, local_count = mesh.shape["node"], mesh.shape["local"]
    x_count = 4 if node_count % 16 == 0 else 2
    column_count = node_count // x_count
    plane_count = x_count * local_count

    def on_device(image, direction, gradient, residual, blocks, block_slot, block_pixel, slot_ray):
        rows_sent = node_count * SEND_CAPACITY
        block_count, held = block_slot.shape[0], slot_ray.shape[0]
        group_blocks = block_count * local_count
        chosen_shape = (local_count, block_count, LANES)

        def f32(*shape):
            return pltpu.VMEM(shape, jnp.float32)

        def pair(send, recv):
            return [f32(*send), f32(*recv)]

        rows, group = (rows_sent, LANES), (group_blocks, LANES)
        scratch = [
            f32(*image.shape), f32(*image.shape), f32(*image.shape), f32(*residual.shape),
            pltpu.VMEM(blocks.shape, jnp.bfloat16), pltpu.VMEM((1, block_count), jnp.int32),
            pltpu.SMEM((1, block_count), jnp.int32), pltpu.VMEM((1, held), jnp.int32),
            pltpu.SemaphoreType.DMA((11,)),
            *pair((1, group_blocks), (local_count, 1, group_blocks)),
            *pair(rows, rows),
            *pair((block_count, LANES), group),
            *pair(rows, rows),
            *pair(rows, rows),
            *pair(group, chosen_shape),
            *pair(rows, rows),
            *pair(group, chosen_shape),
            *pair((2, LANES), (column_count, 2, LANES)),
            *pair((2, LANES), (plane_count, 2, LANES)),
            *pair((1, LANES), (column_count, 1, LANES)),
            *pair((1, LANES), (plane_count, 1, LANES)),
            *[pltpu.SemaphoreType.DMA((4,))] * 6, pltpu.SemaphoreType.REGULAR((2,)),
        ]
        results = pl.pallas_call(
            functools.partial(kernel, (node_count, local_count, x_count)),
            out_shape=tuple(jax.ShapeDtypeStruct(a.shape, jnp.float32) for a in (image, residual, direction)),
            in_specs=[pl.BlockSpec(memory_space=pltpu.HBM)] * 8,
            out_specs=[pl.BlockSpec(memory_space=pltpu.VMEM)] * 3,
            scratch_shapes=scratch,
            compiler_params=pltpu.CompilerParams(
                collective_id=0, has_side_effects=True, vmem_limit_bytes=60 * 1024 * 1024
            ),
        )(
            image, direction, gradient, residual, blocks,
            block_slot.reshape(1, block_count), block_pixel.reshape(1, block_count), slot_ray.reshape(1, held),
        )

        return pl.pallas_call(
            hand_on,
            out_shape=tuple(jax.ShapeDtypeStruct(a.shape, a.dtype) for a in results),
            in_specs=[pl.BlockSpec(memory_space=pltpu.VMEM)] * 3,
            out_specs=[pl.BlockSpec(memory_space=pltpu.VMEM)] * 3,
        )(*results)

    split = P(("node", "local"))
    return jax.shard_map(
        on_device,
        mesh=mesh,
        in_specs=(split,) * 8,
        out_specs=(split,) * 3,
        check_vma=False,
    )
```

```python
import functools

import jax
import jax.numpy as jnp
from jax import lax
from jax.experimental import pallas as pl
from jax.experimental.pallas import tpu as pltpu
from jax.sharding import PartitionSpec as P

SEND_CAPACITY = 2
LANES = 128
MESH = pl.DeviceIdType.MESH
NT = (((1,), (1,)), ((), ()))


def iota(shape, axis):
    return lax.broadcasted_iota(jnp.int32, shape, axis)


def dot(a, b, dims=(((1,), (0,)), ((), ()))):
    return lax.dot_general(a, b, dims, preferred_element_type=jnp.float32)


def one_hot_dot(one_hot, value):
    high = value.astype(jnp.bfloat16)
    rest = value - high.astype(jnp.float32)
    middle = rest.astype(jnp.bfloat16)
    low = (rest - middle.astype(jnp.float32)).astype(jnp.bfloat16)
    width = value.shape[1]
    out = dot(one_hot, jnp.concatenate([high, middle, low], axis=1))
    return out[:, :width] + (out[:, width : 2 * width] + out[:, 2 * width :])


def to_column(row):
    length = row.shape[1]
    square = (length, length)
    return jnp.sum(jnp.where(iota(square, 0) == iota(square, 1), row, 0.0), axis=1, keepdims=True)


def kernel(
    sizes,
    image_hbm, direction_hbm, gradient_hbm, residual_hbm, blocks_hbm, slot_hbm, pixel_hbm, ray_hbm,
    image_out, residual_out, direction_out,
    image, direction, gradient, residual, blocks, slot, pixel, ray, load_sem,
    slot_send, slot_recv, label_send, label_recv,
    contrib_send, contrib_recv, held_send, held_recv,
    reply_send, reply_recv, chosen_send, chosen_recv,
    early_send, early_recv, early_chosen_send, early_chosen_recv,
    norm_a_send, norm_a_recv, norm_b_send, norm_b_recv,
    last_a_send, last_a_recv, last_b_send, last_b_recv,
    y_send_sem, y_recv_sem, n_send_sem, n_recv_sem, s_send_sem, s_recv_sem, round_sem,
):
    node_count, local_count, x_count = sizes
    z_count = node_count // (2 * x_count)
    node = lax.axis_index("node")
    local = lax.axis_index("local")
    x = node // (2 * z_count)
    z = lax.rem(node, 2 * z_count) // 2
    core = lax.rem(node, 2)
    tiles, block_count = image.shape[0], blocks.shape[0]
    held, owned = ray.shape[1], residual.shape[0]
    rows_sent = node_count * SEND_CAPACITY
    group_blocks = block_count * local_count

    def ring(place, size):
        def at(i):
            shift = size // 2 + (i // 2 if i % 2 == 0 else -((i + 1) // 2))
            return place + shift - jnp.where(place + shift >= size, size, 0)

        return [at(i) for i in range(size)]

    x_ring, core_ring, local_ring = ring(x, x_count), ring(core, 2), ring(local, local_count)

    def z_at(i):
        shift = z_count // 2 + jnp.where(lax.rem(i, 2) == 0, i // 2, -((i + 1) // 2))
        return z + shift - jnp.where(z + shift >= z_count, z_count, 0)

    def node_of(x, z, core):
        return (x * z_count + z) * 2 + core

    def along_z(others, body):
        def step(i, carry):
            for other_x, other_core in others:
                body(other_x, z_at(i), other_core)
            return carry

        lax.fori_loop(0, z_count - 1, step, 0)
        for other_x, other_core in others[:-1]:
            body(other_x, z, other_core)

    def of_local(body):
        for other in local_ring[:-1]:
            body(other, (node, other))

    def of_xc(body):
        for other_x, other_core in [(a, b) for a in x_ring for b in core_ring][:-1]:
            body(other_x * 2 + other_core, (node_of(other_x, z, other_core), local))

    def of_z(body):
        along_z([(x, core)], lambda x, z, core: body(z, (node_of(x, z, core), local)))

    def of_node(body):
        def member(x, z, core):
            other = node_of(x, z, core)
            body(other, (other, local))

        along_z([(a, b) for a in x_ring for b in core_ring], member)

    def of_column(body):
        along_z([(x, b) for b in core_ring], lambda x, z, core: body(z * 2 + core, (node_of(x, z, core), local)))

    def of_plane(body):
        for other_local, other_x in [(a, b) for a in local_ring for b in x_ring][:-1]:
            body(other_x * local_count + other_local, (node_of(other_x, z, core), other_local))

    local_group = (local_count, local, of_local)
    node_group = (node_count, node, of_node)
    column_group = (z_count * 2, z * 2 + core, of_column)
    plane_group = (x_count * local_count, x * local_count + local, of_plane)

    barrier = pltpu.get_barrier_semaphore()

    def greet(semaphore):
        return lambda other, device: pl.semaphore_signal(semaphore, inc=1, device_id=device, device_id_type=MESH)

    of_z(greet(barrier))
    of_xc(greet(barrier))
    of_local(greet(barrier))

    chunks = 4
    chunk = block_count // chunks
    loads = {}
    for index, (name, source, target) in enumerate(
        (
            ("ray", ray_hbm, ray),
            ("direction", direction_hbm, direction),
            ("pixel", pixel_hbm, pixel),
            ("slot", slot_hbm, slot),
            *(
                (("blocks", c), blocks_hbm.at[pl.ds(c * chunk, chunk)], blocks.at[pl.ds(c * chunk, chunk)])
                for c in range(chunks)
            ),
            ("gradient", gradient_hbm, gradient),
            ("residual", residual_hbm, residual),
            ("image", image_hbm, image),
        )
    ):
        loads[name] = pltpu.make_async_copy(source, target, load_sem.at[index])
        loads[name].start()

    def exchange(group, source, target, send_sem, recv_sem):
        def send(other, device):
            pltpu.make_async_remote_copy(
                src_ref=source(other), dst_ref=target, send_sem=send_sem, recv_sem=recv_sem,
                device_id=device, device_id_type=MESH,
            ).start()

        group[2](send)
        pltpu.make_async_copy(source(group[1]), target, recv_sem).start()

    def arrived(buffer, recv_sem):
        pltpu.make_async_copy(buffer, buffer, recv_sem).wait()

    loads["direction"].wait()
    loads["pixel"].wait()
    low_direction = direction[...].astype(jnp.bfloat16)
    tile_index = iota((tiles, LANES), 0)
    for c in range(chunks):
        loads["blocks", c].wait()
        chunk_blocks = blocks[pl.ds(c * chunk, chunk)].reshape(chunk * LANES, LANES)
        products = dot(low_direction, chunk_blocks, NT)
        for i in range(chunk):
            b = c * chunk + i
            mine = jnp.where(tile_index == pixel[0, b], products[:, i * LANES : (i + 1) * LANES], 0.0)
            contrib_send[pl.ds(b, 1), :] = jnp.sum(mine, axis=0, keepdims=True)

    pl.semaphore_wait(barrier, local_count + z_count + 2 * x_count - 3)

    my_blocks = pl.ds(pl.multiple_of(local * block_count, block_count), block_count)
    my_rows = pl.ds(node * SEND_CAPACITY, SEND_CAPACITY)

    def rows_of(buffer):
        return lambda other: buffer.at[pl.ds(other * SEND_CAPACITY, SEND_CAPACITY)]

    def blocks_of(buffer):
        return lambda other: buffer.at[pl.ds(pl.multiple_of(other * block_count, block_count), block_count)]

    exchange(local_group, lambda other: contrib_send, contrib_recv.at[my_blocks], y_send_sem.at[1], y_recv_sem.at[1])
    loads["slot"].wait()
    slot_row = jnp.concatenate([slot[...].astype(jnp.float32)] * local_count, axis=1)
    slot_send[...] = jnp.where(iota(slot_row.shape, 1) // block_count == local, slot_row, 0.0)

    exchange(local_group, lambda other: slot_send, slot_recv.at[local], y_send_sem.at[0], y_recv_sem.at[0])
    of_z(greet(round_sem.at[0]))
    of_local(greet(round_sem.at[1]))
    loads["ray"].wait()
    rays = ray[...]
    target_node = lax.div(rays, owned * local_count).astype(jnp.float32)
    tile = lax.rem(rays, owned).astype(jnp.float32)
    square = (held, held)
    standing = jnp.sum(
        jnp.where((to_column(target_node) == target_node) & (iota(square, 0) < iota(square, 1)), 1.0, 0.0),
        axis=0,
        keepdims=True,
    )
    position = target_node * SEND_CAPACITY + standing
    spread = (iota((rows_sent, held), 0).astype(jnp.float32) == position).astype(jnp.bfloat16)
    tile_one_hot = (iota((held, LANES), 1).astype(jnp.float32) == to_column(tile)).astype(jnp.bfloat16)
    label_send[...] = dot(spread, tile_one_hot)

    pl.semaphore_wait(round_sem.at[0], z_count - 1)
    exchange(node_group, rows_of(label_send), label_recv.at[my_rows], n_send_sem.at[0], n_recv_sem.at[0])

    arrived(slot_recv, y_recv_sem.at[0])
    group_slot = jnp.sum(slot_recv[...], axis=0) - (local * held).astype(jnp.float32)
    in_slot = (iota((held, group_blocks), 0).astype(jnp.float32) == group_slot).astype(jnp.bfloat16)
    of_slot = (iota((group_blocks, held), 1).astype(jnp.float32) == to_column(group_slot)).astype(jnp.bfloat16)
    gather_rows = dot(spread, in_slot).astype(jnp.bfloat16)
    scatter_rows = dot(of_slot, spread, NT).astype(jnp.bfloat16)

    arrived(contrib_recv, y_recv_sem.at[1])
    held_send[...] = one_hot_dot(gather_rows, contrib_recv[...])
    exchange(node_group, rows_of(held_send), held_recv.at[my_rows], n_send_sem.at[1], n_recv_sem.at[1])

    arrived(label_recv, n_recv_sem.at[0])
    labels = label_recv[...].astype(jnp.bfloat16)
    tile_square = (iota((owned, LANES), 0) == iota((owned, LANES), 1)).astype(jnp.bfloat16)
    collect = dot(tile_square, labels, NT).astype(jnp.bfloat16)
    labels_owned = labels[:, :owned]
    same_tile = dot(labels_owned, collect).astype(jnp.bfloat16)
    loads["residual"].wait()
    early_send[...] = one_hot_dot(labels_owned, residual[...])
    exchange(node_group, rows_of(early_send), early_recv.at[my_rows], n_send_sem.at[2], n_recv_sem.at[2])

    loads["gradient"].wait()
    loads["image"].wait()
    old_norm_row = jnp.sum(gradient[...] * gradient[...], axis=0, keepdims=True)

    arrived(held_recv, n_recv_sem.at[1])
    reply_send[...] = one_hot_dot(same_tile, held_recv[...])
    projected = one_hot_dot(collect, held_recv[...])
    norm_a_send[0:1, :] = jnp.sum(projected * projected, axis=0, keepdims=True)
    norm_a_send[1:2, :] = old_norm_row
    exchange(column_group, lambda other: norm_a_send, norm_a_recv.at[column_group[1]], s_send_sem.at[0], s_recv_sem.at[0])
    exchange(node_group, rows_of(reply_send), reply_recv.at[my_rows], n_send_sem.at[3], n_recv_sem.at[3])

    arrived(early_recv, n_recv_sem.at[2])
    early_chosen_send[...] = one_hot_dot(scatter_rows, early_recv[...])
    exchange(
        local_group, blocks_of(early_chosen_send), early_chosen_recv.at[local], y_send_sem.at[2], y_recv_sem.at[2]
    )

    arrived(norm_a_recv, s_recv_sem.at[0])
    norm_b_send[...] = jnp.sum(norm_a_recv[...], axis=0)
    me_in_plane = plane_group[1]
    pl.semaphore_wait(round_sem.at[1], local_count - 1)
    exchange(plane_group, lambda other: norm_b_send, norm_b_recv.at[me_in_plane], s_send_sem.at[1], s_recv_sem.at[1])

    arrived(reply_recv, n_recv_sem.at[3])
    chosen_send[...] = one_hot_dot(scatter_rows, reply_recv[...])
    exchange(local_group, blocks_of(chosen_send), chosen_recv.at[local], y_send_sem.at[3], y_recv_sem.at[3])

    arrived(norm_b_recv, s_recv_sem.at[1])
    norms = jnp.sum(norm_b_recv[...], axis=0)
    curvature = jnp.sum(norms[0:1, :], axis=1, keepdims=True)
    old_norm = jnp.sum(norms[1:2, :], axis=1, keepdims=True)
    step_size = old_norm / curvature
    image_out[...] = image[...] + step_size * direction[...]
    residual_out[...] = residual[...] - step_size * projected

    arrived(early_chosen_recv, y_recv_sem.at[2])
    old_chosen = jnp.sum(early_chosen_recv[...], axis=0)
    arrived(chosen_recv, y_recv_sem.at[3])
    chosen = old_chosen - step_size * jnp.sum(chosen_recv[...], axis=0)

    gradient_new = jnp.zeros((tiles, LANES), jnp.float32)
    for c in range(chunks):
        spread_residual = jnp.concatenate(
            [
                jnp.where(tile_index == pixel[0, b], chosen[b : b + 1, :], 0.0)
                for b in range(c * chunk, (c + 1) * chunk)
            ],
            axis=1,
        ).astype(jnp.bfloat16)
        chunk_blocks = blocks[pl.ds(c * chunk, chunk)].reshape(chunk * LANES, LANES)
        gradient_new += dot(spread_residual, chunk_blocks)

    last_a_send[...] = jnp.sum(gradient_new * gradient_new, axis=0, keepdims=True)
    exchange(column_group, lambda other: last_a_send, last_a_recv.at[column_group[1]], s_send_sem.at[2], s_recv_sem.at[2])
    arrived(last_a_recv, s_recv_sem.at[2])
    last_b_send[...] = jnp.sum(last_a_recv[...], axis=0)
    exchange(plane_group, lambda other: last_b_send, last_b_recv.at[me_in_plane], s_send_sem.at[3], s_recv_sem.at[3])
    arrived(last_b_recv, s_recv_sem.at[3])
    new_norm = jnp.sum(jnp.sum(last_b_recv[...], axis=0), axis=1, keepdims=True)
    direction_out[...] = gradient_new + (new_norm / old_norm) * direction[...]

    def sent(group, buffer, each_rows, send_sem):
        sample = buffer.at[pl.ds(0, (group[0] - 1) * each_rows)]
        pltpu.make_async_copy(sample, sample, send_sem).wait()

    sent(local_group, slot_recv, 1, y_send_sem.at[0])
    sent(local_group, contrib_recv, block_count, y_send_sem.at[1])
    sent(local_group, early_chosen_recv, 1, y_send_sem.at[2])
    sent(local_group, chosen_recv, 1, y_send_sem.at[3])
    for index, buffer in enumerate((label_recv, held_recv, early_recv, reply_recv)):
        sent(node_group, buffer, SEND_CAPACITY, n_send_sem.at[index])
    sent(column_group, norm_a_recv, 1, s_send_sem.at[0])
    sent(plane_group, norm_b_recv, 1, s_send_sem.at[1])
    sent(column_group, last_a_recv, 1, s_send_sem.at[2])
    sent(plane_group, last_b_recv, 1, s_send_sem.at[3])


def hand_on(*refs):
    arrays = len(refs) // 2
    for i in range(arrays):
        refs[arrays + i][...] = refs[i][...]


def solution(mesh):
    node_count, local_count = mesh.shape["node"], mesh.shape["local"]
    x_count = 4 if node_count % 16 == 0 else 2
    column_count = node_count // x_count
    plane_count = x_count * local_count

    def on_device(image, direction, gradient, residual, blocks, block_slot, block_pixel, slot_ray):
        rows_sent = node_count * SEND_CAPACITY
        block_count, held = block_slot.shape[0], slot_ray.shape[0]
        group_blocks = block_count * local_count
        chosen_shape = (local_count, block_count, LANES)

        def f32(*shape):
            return pltpu.VMEM(shape, jnp.float32)

        def pair(send, recv):
            return [f32(*send), f32(*recv)]

        rows, group = (rows_sent, LANES), (group_blocks, LANES)
        scratch = [
            f32(*image.shape), f32(*image.shape), f32(*image.shape), f32(*residual.shape),
            pltpu.VMEM(blocks.shape, jnp.bfloat16), pltpu.VMEM((1, block_count), jnp.int32),
            pltpu.SMEM((1, block_count), jnp.int32), pltpu.VMEM((1, held), jnp.int32),
            pltpu.SemaphoreType.DMA((11,)),
            *pair((1, group_blocks), (local_count, 1, group_blocks)),
            *pair(rows, rows),
            *pair((block_count, LANES), group),
            *pair(rows, rows),
            *pair(rows, rows),
            *pair(group, chosen_shape),
            *pair(rows, rows),
            *pair(group, chosen_shape),
            *pair((2, LANES), (column_count, 2, LANES)),
            *pair((2, LANES), (plane_count, 2, LANES)),
            *pair((1, LANES), (column_count, 1, LANES)),
            *pair((1, LANES), (plane_count, 1, LANES)),
            *[pltpu.SemaphoreType.DMA((4,))] * 6, pltpu.SemaphoreType.REGULAR((2,)),
        ]
        results = pl.pallas_call(
            functools.partial(kernel, (node_count, local_count, x_count)),
            out_shape=tuple(jax.ShapeDtypeStruct(a.shape, jnp.float32) for a in (image, residual, direction)),
            in_specs=[pl.BlockSpec(memory_space=pltpu.HBM)] * 8,
            out_specs=[pl.BlockSpec(memory_space=pltpu.VMEM)] * 3,
            scratch_shapes=scratch,
            compiler_params=pltpu.CompilerParams(
                collective_id=0, has_side_effects=True, vmem_limit_bytes=60 * 1024 * 1024
            ),
        )(
            image, direction, gradient, residual, blocks,
            block_slot.reshape(1, block_count), block_pixel.reshape(1, block_count), slot_ray.reshape(1, held),
        )

        return pl.pallas_call(
            hand_on,
            out_shape=tuple(jax.ShapeDtypeStruct(a.shape, a.dtype) for a in results),
            in_specs=[pl.BlockSpec(memory_space=pltpu.VMEM)] * 3,
            out_specs=[pl.BlockSpec(memory_space=pltpu.VMEM)] * 3,
        )(*results)

    split = P(("node", "local"))
    return jax.shard_map(
        on_device,
        mesh=mesh,
        in_specs=(split,) * 8,
        out_specs=(split,) * 3,
        check_vma=False,
    )
```
